32 devices in a mesh: section: 2 (over core), seq: 8 (over z, x), mp: 2 (over y).
Axes of the slice: x: 2, y: 2, z: 4, core: 2. Of those that a mesh axis runs over, the one named last changes fastest.
Arguments:
- patches: bfloat16 [4096, 1280], P(('section', 'seq')), may hold values from -6 to 6
- inner_weight: bfloat16 [3, 1280, 1280], P(None, None, 'mp'), may hold values from -0.15625 to 0.15625
- norm_gain: float32 [1280], replicated, may hold values from 0.5 to 12
- outer_weight: bfloat16 [1280, 1280], P('mp'), may hold values from -0.15625 to 0.15625
- merge_gain: float32 [1280], replicated, may hold values from 0.5 to 1.5
- windows: int32 [16, 256], P(('section', 'seq')), may hold values from 0 to 7, never falling along the last dimension, each value on 1 to 64 neighbouring positions
- owners: int32 [1024, 1], P(('section', 'seq')), may hold values from 0 to 15; in each aligned block of 64 rows (0 to 63, 64 to 127, ...) at most 16 rows name the same one
- context_query: bfloat16 [1024, 8192], P('seq', ('section', 'mp')), may hold values from -150 to 150
- context_key: bfloat16 [1024, 1024], P('seq', ('section', 'mp')), may hold values from -6 to 6
- context_value: bfloat16 [1024, 1024], P('seq', ('section', 'mp')), may hold values from -6 to 6
- documents: int32 [1024], replicated, may hold values from 0 to 7, never falling along the last dimension, each value on 1 to 768 neighbouring positions
Outputs:
- delivered: bfloat16 [4096, 5120], P(('section', 'seq'), 'mp')
- attended: bfloat16 [1024, 8192], P('seq', ('section', 'mp'))
The draws below stay inside these ranges and needn't reach their ends.
Inputs may be any that keep to these rules, and one draw needn't show every extreme that they name: Along each row the window numbers never fall, and each of the 8 windows holds 1 to 64 patches. `owners`: among the 64 tokens of one device (aligned blocks of rows) no owner is named more than 16 times; some owner is named exactly 16 times in some blocks. Document numbers never fall; each of the 8 documents holds 1 to 768 positions, one exactly 768.
All inputs are finite; a program needn't handle non-finite values.
Results may differ from the reference program's by a relative error of at most 0.012.
The reference program's roundings to bfloat16 on the way count: a program that leaves them out, or rounds other values in their place, can miss the bound.
Values may be sent and summed in bfloat16 or wider, within the bound.
A program may use at most 128 MiB of HBM per device.

```python
import math
import jax
import jax.numpy as jnp
import numpy as np
from jax import lax

VD = 1280
VH = 16
QH = 64
KVH = 8
HD = 128
P_DEV = 256
WIN_MOST = 64
DOCS = 8
OWNERS = 16
PATCHES = 4096
TOK_DEV = 64
MERGED = 1024
CAP = 16
WINS = 8
CONTEXT = 1024
DOC_MOST = 768


def draw_norm_gain(key, part):
    uniform_part = jax.random.uniform(jax.random.fold_in(key, 3), (VD,), jnp.float32)
    lowest, highest = (0.5, 2.0)
    return jnp.exp(jnp.log(lowest) + uniform_part * (jnp.log(highest) - jnp.log(lowest)))


def paired_draw(key):
    query_seed = jax.random.fold_in(key, 101)
    key_seed = jax.random.fold_in(key, 102)
    key_heads = jnp.clip(jax.random.normal(key_seed, (CONTEXT, KVH, HD), jnp.float32), -5.0, 5.0)
    query_heads = jnp.clip(3.0 * jax.random.normal(query_seed, (CONTEXT, QH, HD), jnp.float32), -15.0, 15.0)
    return (query_heads.reshape(CONTEXT, QH * HD), key_heads.reshape(CONTEXT, KVH * HD))


def draw_context_query(key, part):
    return paired_draw(key)[0].astype(jnp.bfloat16)


def draw_context_key(key, part):
    return paired_draw(key)[1].astype(jnp.bfloat16)


def level_of(key, extent, split, low, high):
    level = 1.0
    for axis_at, shards_of in split:
        heights = jax.random.uniform(jax.random.fold_in(jax.random.fold_in(key, 6), axis_at), (shards_of,), jnp.float32, low / len(split), high / len(split))
        level = level * jnp.repeat(jnp.exp(heights), extent[axis_at] // shards_of).reshape((-1,) + (1,) * (len(extent) - 1 - axis_at))
    return level


def length_profile(count, total, most, slope):
    portions = [(1 << 20) // math.isqrt(grade ** slope) + 1 for grade in range(2, count + 1)]
    surplus, given = total - most - (count - 1), [1] * (count - 1)
    while surplus > 0:
        candidates = [i for i in range(count - 1) if given[i] < most]
        mass, budget = sum([portions[i] for i in candidates]), surplus
        for i in candidates:
            extra = min(most - given[i], max(1, budget * portions[i] // mass), surplus)
            given[i] = given[i] + extra
            surplus = surplus - extra
    return np.array([most] + given)


def ragged_sizes(rng, number_of, total, bound, slope):
    if number_of == 2:
        one = jax.random.randint(rng, (), max(1, total - bound), min(bound, total - 1) + 1)
        return jnp.stack([one, total - one])
    lengths = jnp.asarray(length_profile(number_of, total, bound, slope), jnp.int32)
    couples = (number_of - 1) // 2
    giver, sink = lengths[1:1 + 2 * couples:2], lengths[2:2 + 2 * couples:2]
    margin = jnp.minimum(giver - 1, bound - sink)
    shifted = jax.random.randint(jax.random.fold_in(rng, 1), (couples,), 0, 1 << 20) % (margin + 1)
    lengths = lengths.at[1:1 + 2 * couples:2].set(giver - shifted).at[2:2 + 2 * couples:2].set(sink + shifted)
    return lengths[jax.random.permutation(jax.random.fold_in(rng, 2), number_of)]


def shared_out(stream_key, own, number, rows, count, top, limit, lean):
    order = jax.random.permutation(stream_key, count)
    crowded, common = shares(count, rows * top, limit, lean, True), shares(count, rows * top, limit, lean, False)
    places = jnp.arange(count)

    def named(lengths, turn):
        used = int((lengths > 0).sum())
        fixed = max(1, used // 4)
        moved = fixed + (places - fixed + turn * (used - fixed)) % max(1, count - fixed)
        return jnp.zeros((count,), jnp.int32).at[order[jnp.where(places < fixed, places, moved)]].set(jnp.asarray(lengths, jnp.int32))

    lengths = jnp.where(number % 4 == 0, named(crowded, number // 4), named(common, number - number // 4 - 1))
    mixed = jax.random.permutation(jax.random.fold_in(own, 3), count)
    giver, taker = mixed[0:count // 2 * 2:2], mixed[1:count // 2 * 2:2]
    room = jnp.minimum(lengths[giver] - 1, limit - lengths[taker]) // 2
    room = jnp.where((giver == order[0]) | (taker == order[0]) | (lengths[taker] == 0), 0, jnp.maximum(room, 0))
    moved = jax.random.randint(jax.random.fold_in(own, 4), (count // 2,), 0, 1 << 20) % (room + 1)
    lengths = lengths.at[giver].add(-moved).at[taker].add(moved)
    members = jnp.searchsorted(jnp.cumsum(lengths), jnp.arange(rows * top), side="right").astype(jnp.int32)
    table = members.reshape(top, rows).T
    table = table[jax.random.permutation(jax.random.fold_in(own, 1), rows)]
    turn = jax.random.randint(jax.random.fold_in(own, 2), (rows, 1), 0, top)
    return jnp.take_along_axis(table, (jnp.arange(top)[None, :] + turn) % top, axis=1)


def shares(count, total, reach, lean, full):
    portions = [(1 << 20) // math.isqrt(grade ** lean) + 1 for grade in range(1, count + 1)]
    largest = reach if full else min(reach, max(-(-total // count), total * portions[0] // sum(portions)))
    least = 1 if total - largest >= count - 1 else 0
    holding, spare = [largest] + [least] * (count - 1), total - largest - least * (count - 1)
    while spare > 0:
        candidates = [i for i in range(1, count) if holding[i] < largest] or [i for i in range(1, count) if holding[i] < reach]
        whole, remaining = sum([portions[i] for i in candidates]), spare
        for i in candidates:
            more = min(reach - holding[i], max(1, remaining * portions[i] // whole), spare)
            holding[i] = holding[i] + more
            spare = spare - more
    return np.array(holding)


def scatter_about(stream_key, shape, width, most, cuts=(), kind=jnp.bfloat16):
    result = jax.random.normal(stream_key, shape, jnp.float32) * width
    if len(cuts) > 0:
        result = level_of(stream_key, shape, cuts, -0.22, 0.18) * result
    return jnp.clip(result, min=-most, max=most).astype(kind)


def setup_inputs(seed: int = 0) -> dict:
    streams_of = jax.random.split(jax.random.key(seed), 12)
    patches = scatter_about(streams_of[0], (PATCHES, VD), 1.0, 6.0, ((0, 16),))
    inner_weight = scatter_about(streams_of[1], (3, VD, VD), VD ** -0.5, 0.15625, ((2, 2),))
    norm_gain = draw_norm_gain(jax.random.fold_in(streams_of[11], 71), 0)
    outer_weight = scatter_about(streams_of[3], (VD, VD), VD ** -0.5, 0.15625, ((0, 2),))
    merge_gain = jnp.clip(1.0 + 0.1 * jax.random.normal(streams_of[4], (VD,), jnp.float32), 0.5, 1.5)
    windows = jax.vmap(lambda own: jnp.searchsorted(jnp.cumsum(ragged_sizes(own, WINS, P_DEV, WIN_MOST, 0)), jnp.arange(P_DEV), side="right"))(jax.random.split(streams_of[5], OWNERS)).reshape((OWNERS, P_DEV)).astype(jnp.int32)
    owners_keys = jax.random.split(jax.random.fold_in(streams_of[6], 1), MERGED // TOK_DEV)
    owners_turns = jax.random.permutation(jax.random.fold_in(streams_of[6], 3), MERGED // TOK_DEV)
    owners = jax.vmap(lambda own, number: shared_out(jax.random.fold_in(streams_of[6], 2), own, number, TOK_DEV, OWNERS, 1, CAP, 2))(owners_keys, owners_turns).reshape((MERGED, 1))
    context_query = draw_context_query(jax.random.fold_in(streams_of[11], 71), 0)
    context_key = draw_context_key(jax.random.fold_in(streams_of[11], 71), 0)
    context_value = scatter_about(streams_of[9], (CONTEXT, KVH * HD), 1.0, 6.0, ((0, 8), (1, 4)))
    documents = jnp.searchsorted(jnp.cumsum(ragged_sizes(streams_of[10], DOCS, CONTEXT, DOC_MOST, 1)), jnp.arange(CONTEXT), side="right").astype(jnp.int32)
    return {"patches": patches, "inner_weight": inner_weight, "norm_gain": norm_gain, "outer_weight": outer_weight, "merge_gain": merge_gain, "windows": windows, "owners": owners, "context_query": context_query, "context_key": context_key, "context_value": context_value, "documents": documents}


EPSILON = 1e-06

def rms_scale(values, gain):
    return values * lax.rsqrt(lax.optimization_barrier(jnp.mean(values * values, axis=-1, keepdims=True)) + EPSILON) * gain

def settle(values):
    return lax.optimization_barrier(values.astype(jnp.bfloat16)).astype(jnp.float32)

def vision_merge(patches, inner_weight, norm_gain, outer_weight, merge_gain, windows):
    head_dim = VD // VH

    def one_block(inputs):
        patch_block, window_row = inputs
        source = patch_block.astype(jnp.float32)
        normed = rms_scale(source, norm_gain).astype(jnp.bfloat16)
        query_heads = settle(jnp.dot(normed, inner_weight[0], preferred_element_type=jnp.float32)).reshape(P_DEV, VH, head_dim)
        key_heads = settle(jnp.dot(normed, inner_weight[1], preferred_element_type=jnp.float32)).reshape(P_DEV, VH, head_dim)
        value_heads = settle(jnp.dot(normed, inner_weight[2], preferred_element_type=jnp.float32)).reshape(P_DEV, VH, head_dim)
        scores = jnp.einsum('qhd,khd->hqk', query_heads, key_heads) / math.sqrt(head_dim)
        allowed = window_row[:, None] == window_row[None, :]
        scores = jnp.where(allowed[None], scores, -jnp.inf)
        row_peak = lax.optimization_barrier(jnp.max(scores, axis=-1, keepdims=True))
        weights = jnp.exp(scores - row_peak)
        denominator = lax.optimization_barrier(jnp.sum(weights, axis=-1))
        context = jnp.einsum('hqk,khd->qhd', settle(weights), value_heads)
        context = (context / jnp.transpose(denominator)[:, :, None]).astype(jnp.bfloat16).reshape(P_DEV, VD)
        residual = source + jnp.dot(context, outer_weight, preferred_element_type=jnp.float32)
        merged = rms_scale(residual, merge_gain).astype(jnp.bfloat16)
        return merged.reshape(P_DEV // 4, 4 * VD)
    blocks = lax.map(one_block, (patches.reshape(OWNERS, P_DEV, VD), windows))
    return blocks.reshape(MERGED, 4 * VD)

def place_tokens(merged, owners):
    target = owners[:, 0].reshape(OWNERS, TOK_DEV)
    order = jnp.arange(TOK_DEV, dtype=jnp.int32)
    earlier = order[None, :] < order[:, None]
    slot_rank = lax.optimization_barrier(jnp.sum((target[:, :, None] == target[:, None, :]) & earlier[None], axis=2)).astype(jnp.int32)
    source_block = jnp.arange(OWNERS, dtype=jnp.int32)[:, None]
    destination = ((target * OWNERS + source_block) * CAP + slot_rank).reshape(MERGED).astype(jnp.int32)
    empty = jnp.zeros((OWNERS * OWNERS * CAP, 4 * VD), jnp.bfloat16)
    return empty.at[destination].set(merged)

def context_attention(context_query, context_key, context_value, documents):
    groups = QH // KVH
    key_heads = context_key.astype(jnp.float32).reshape(CONTEXT, KVH, HD)
    value_heads = context_value.astype(jnp.float32).reshape(CONTEXT, KVH, HD)
    positions = jnp.arange(CONTEXT, dtype=jnp.int32)
    query_block = math.gcd(CONTEXT, 256)

    def one_block(offset):
        query_heads = lax.dynamic_slice_in_dim(context_query, offset, query_block, 0).astype(jnp.float32)
        query_heads = query_heads.reshape(query_block, KVH, groups, HD)
        scores = jnp.einsum('qhgd,khd->hgqk', query_heads, key_heads) / math.sqrt(HD)
        query_positions = offset + jnp.arange(query_block, dtype=jnp.int32)
        query_docs = lax.dynamic_slice_in_dim(documents, offset, query_block, 0)
        allowed = (positions[None, :] <= query_positions[:, None]) & (documents[None, :] == query_docs[:, None])
        scores = jnp.where(allowed[None, None], scores, -jnp.inf)
        row_peak = lax.optimization_barrier(jnp.max(scores, axis=-1, keepdims=True))
        weights = jnp.exp(scores - row_peak)
        denominator = lax.optimization_barrier(jnp.sum(weights, axis=-1))
        output = jnp.einsum('hgqk,khd->qhgd', settle(weights), value_heads)
        output = output / jnp.transpose(denominator, (2, 0, 1))[..., None]
        return output.astype(jnp.bfloat16).reshape(query_block, QH * HD)
    starts = (jnp.arange(CONTEXT // query_block, dtype=jnp.int32) * query_block).astype(jnp.int32)
    return lax.map(one_block, starts).reshape(CONTEXT, QH * HD)

def reference(patches, inner_weight, norm_gain, outer_weight, merge_gain, windows, owners, context_query, context_key, context_value, documents):
    merged = vision_merge(patches, inner_weight, norm_gain, outer_weight, merge_gain, windows)
    delivered = place_tokens(merged, owners)
    attended = context_attention(context_query, context_key, context_value, documents)
    return (delivered, attended)
```

```python
import functools
import math

import jax
import jax.numpy as jnp
from jax import lax
from jax.experimental import pallas as pl
from jax.experimental.pallas import tpu as pltpu
from jax.sharding import PartitionSpec as P

VD = 1280
VH = 16
QH = 64
KVH = 8
HD = 128
EPSILON = 1e-06
LOG2E = 1.4426950408889634
MESH = pl.DeviceIdType.MESH
F32 = jnp.float32
BF16 = jnp.bfloat16


def rms_scale(values, gain):
    return values * lax.rsqrt(jnp.mean(values * values, axis=-1, keepdims=True) + EPSILON) * gain


def row_to_column(row, size):
    spread = jnp.broadcast_to(row, (size, size))
    eye = lax.broadcasted_iota(jnp.int32, (size, size), 0) == lax.broadcasted_iota(
        jnp.int32, (size, size), 1
    )
    return jnp.sum(jnp.where(eye, spread, 0.0), axis=1, keepdims=True)


def kernel(
    sections,
    seqs,
    capacity,
    patches_ref,
    inner_hbm,
    norm_ref,
    outer_hbm,
    merge_ref,
    window_ref,
    owner_ref,
    query_hbm,
    key_hbm,
    value_hbm,
    doc_ref,
    delivered_hbm,
    attended_ref,
    inner_buf,
    outer_buf,
    query_buf,
    kv,
    normed_buf,
    qkv_buf,
    ctx_buf,
    part_send,
    part_recv,
    outgoing,
    load_sem,
    kv_recv,
    chain_send,
    side_send,
    part_sem,
    out_send,
    out_recv,
):
    section, seq, mp = lax.axis_index("section"), lax.axis_index("seq"), lax.axis_index("mp")
    owner_count = sections * seqs
    me = section * seqs + seq
    rows = patches_ref.shape[0]
    width = patches_ref.shape[1]
    tokens = rows // 4
    head_dim = VD // VH
    local = inner_hbm.shape[2]
    local_heads = local // head_dim
    half = rows // 2

    def at(sec, sq, m):
        return {"section": sec, "seq": sq, "mp": m}

    loads = [
        pltpu.make_async_copy(key_hbm, kv.at[seq, 0], load_sem.at[0]),
        pltpu.make_async_copy(value_hbm, kv.at[seq, 1], load_sem.at[1]),
        pltpu.make_async_copy(inner_hbm.at[0], inner_buf.at[0], load_sem.at[2]),
        pltpu.make_async_copy(inner_hbm.at[1], inner_buf.at[1], load_sem.at[3]),
        pltpu.make_async_copy(inner_hbm.at[2], inner_buf.at[2], load_sem.at[4]),
        pltpu.make_async_copy(outer_hbm, outer_buf, load_sem.at[5]),
        pltpu.make_async_copy(query_hbm, query_buf, load_sem.at[6]),
    ]
    for load in loads:
        load.start()

    barrier = pltpu.get_barrier_semaphore()

    def greet(k, carry):
        other = lax.rem(me + k, owner_count)
        pl.semaphore_signal(
            barrier,
            inc=1,
            device_id=at(other // seqs, lax.rem(other, seqs), mp),
            device_id_type=MESH,
        )
        return carry

    lax.fori_loop(1, owner_count, greet, 0)
    pl.semaphore_signal(
        barrier, inc=1, device_id=at(section, seq, 1 - mp), device_id_type=MESH
    )

    def clear(j, carry):
        kv[j] = jnp.zeros(kv.shape[1:], BF16)
        return carry

    lax.fori_loop(seq + 1, seqs, clear, 0)

    pl.semaphore_wait(barrier, owner_count)

    side = seq + 1 - 2 * lax.rem(seq, 2)

    def chain_copy(j):
        block = seq - 2 * j
        return pltpu.make_async_remote_copy(
            src_ref=kv.at[block],
            dst_ref=kv.at[block],
            send_sem=chain_send.at[j],
            recv_sem=kv_recv.at[block],
            device_id=at(section, seq + 2, mp),
            device_id_type=MESH,
        )

    def side_copy(j):
        block = seq - 2 * j
        return pltpu.make_async_remote_copy(
            src_ref=kv.at[block],
            dst_ref=kv.at[block],
            send_sem=side_send.at[j],
            recv_sem=kv_recv.at[block],
            device_id=at(section, side, mp),
            device_id_type=MESH,
        )

    def arrived(block):
        return pltpu.make_async_copy(kv.at[block], kv.at[block], kv_recv.at[block])

    loads[0].wait()
    loads[1].wait()

    @pl.when(seq + 2 < seqs)
    def _():
        chain_copy(0).start()

    @pl.when(lax.rem(seq, 2) == 0)
    def _():
        side_copy(0).start()

    def relay(j, carry):
        @pl.when(seq - 2 * j >= 0)
        def _():
            arrived(seq - 2 * j).wait()

            @pl.when(seq + 2 < seqs)
            def _():
                chain_copy(j).start()

            side_copy(j).start()

        return carry

    hops = seqs // 2
    first_hops = 1 + (hops - 1) // 3
    second_hops = 1 + 2 * (hops - 1) // 3

    normed_buf[...] = rms_scale(patches_ref[...].astype(F32), norm_ref[...]).astype(BF16)
    for i in range(3):
        loads[2 + i].wait()
        qkv_buf[i] = jnp.dot(
            normed_buf[...], inner_buf[i], preferred_element_type=F32
        ).astype(BF16)

    lax.fori_loop(1, first_hops, relay, 0)

    window_row = window_ref[...].astype(F32)
    allowed = row_to_column(window_row, rows) == window_row
    score_scale = LOG2E / math.sqrt(head_dim)
    ctx = [jnp.zeros((rows, 128), F32) for _ in range(local // 128)]
    for h in range(local_heads):
        low, high = h * head_dim, (h + 1) * head_dim
        first, last = low // 128, -(-high // 128)
        span = pl.ds(first * 128, (last - first) * 128)
        lanes = first * 128 + lax.broadcasted_iota(jnp.int32, (1, (last - first) * 128), 1)
        inside = (lanes >= low) & (lanes < high)
        query = jnp.where(inside, qkv_buf[0, :, span], jnp.zeros((), BF16))
        scores = lax.dot_general(
            query, qkv_buf[1, :, span], (((1,), (1,)), ((), ())), preferred_element_type=F32
        )
        scores = jnp.where(allowed, scores, -jnp.inf)
        peak = jnp.max(scores, axis=-1, keepdims=True)
        weights = jnp.exp2((scores - peak) * score_scale)
        denominator = jnp.sum(weights, axis=-1, keepdims=True)
        part = jnp.dot(weights.astype(BF16), qkv_buf[2, :, span], preferred_element_type=F32)
        part = jnp.where(inside, part / denominator, 0.0)
        for i in range(first, last):
            ctx[i] = ctx[i] + part[:, (i - first) * 128 : (i - first + 1) * 128]
    for i in range(local // 128):
        ctx_buf[:, i * 128 : (i + 1) * 128] = ctx[i].astype(BF16)

    lax.fori_loop(first_hops, second_hops, relay, 0)

    place = lax.broadcasted_iota(jnp.int32, (half, rows), 0)
    source_at = lax.broadcasted_iota(jnp.int32, (half, rows), 1)

    def chosen(m):
        wanted = 4 * lax.rem(place, tokens) + 2 * m + place // tokens
        return jnp.where(source_at == wanted, 1.0, 0.0).astype(BF16)

    loads[5].wait()
    theirs = jnp.dot(chosen(1 - mp), ctx_buf[...], preferred_element_type=F32).astype(BF16)
    part_send[...] = jnp.dot(theirs, outer_buf[...], preferred_element_type=F32).astype(BF16)
    part_copy = pltpu.make_async_remote_copy(
        src_ref=part_send,
        dst_ref=part_recv,
        send_sem=part_sem.at[0],
        recv_sem=part_sem.at[1],
        device_id=at(section, seq, 1 - mp),
        device_id_type=MESH,
    )
    part_copy.start()
    pick = chosen(mp)
    ours = jnp.dot(pick, ctx_buf[...], preferred_element_type=F32).astype(BF16)
    own_part = jnp.dot(ours, outer_buf[...], preferred_element_type=F32)
    own_part = own_part + jnp.dot(pick, patches_ref[...], preferred_element_type=F32)

    owner_spread = jnp.broadcast_to(owner_ref[...].astype(F32), (tokens, tokens))
    earlier_at = lax.broadcasted_iota(jnp.int32, (tokens, tokens), 0)
    later_at = lax.broadcasted_iota(jnp.int32, (tokens, tokens), 1)
    owner_row = jnp.sum(
        jnp.where(earlier_at == later_at, owner_spread, 0.0), axis=0, keepdims=True
    )
    rank_row = jnp.sum(
        jnp.where((owner_spread == owner_row) & (earlier_at < later_at), 1.0, 0.0),
        axis=0,
        keepdims=True,
    )
    slot_row = (owner_row * capacity + rank_row).astype(jnp.int32)
    slot_at = lax.broadcasted_iota(jnp.int32, (capacity, tokens), 0)

    lax.fori_loop(second_hops, hops, relay, 0)

    part_copy.wait_recv()
    residual = own_part + part_recv[...].astype(F32)
    normed_buf[0:half, :] = rms_scale(residual, merge_ref[...]).astype(BF16)

    def out_copy(owner):
        return pltpu.make_async_remote_copy(
            src_ref=outgoing.at[owner],
            dst_ref=delivered_hbm.at[me],
            send_sem=out_send.at[owner],
            recv_sem=out_recv.at[me],
            device_id=at(owner // seqs, lax.rem(owner, seqs), mp),
            device_id_type=MESH,
        )

    def fill(owner):
        spot = jnp.where(slot_at + owner * capacity == slot_row, 1.0, 0.0).astype(BF16)
        for g in range(2):
            outgoing[owner, :, g * width : (g + 1) * width] = jnp.dot(
                spot,
                normed_buf[g * tokens : (g + 1) * tokens, :],
                preferred_element_type=F32,
            ).astype(BF16)

    def send_out(k, carry):
        owner = lax.rem(me + k, owner_count)
        fill(owner)
        out_copy(owner).start()
        return carry

    lax.fori_loop(1, owner_count, send_out, 0)
    fill(me)
    keep = pltpu.make_async_copy(outgoing.at[me], delivered_hbm.at[me], out_send.at[me])
    keep.start()

    def side_arrival(j, carry):
        block = side - 2 * j

        @pl.when((block >= 0) & (block < seq))
        def _():
            arrived(block).wait()

        return carry

    lax.fori_loop(0, hops, side_arrival, 0)
    loads[6].wait()

    query_rows = query_buf.shape[0]
    context = doc_ref.shape[1]
    groups = QH // KVH
    heads = query_buf.shape[1] // HD
    together = max(1, min(4, (512 * 1024) // (query_rows * context)))
    first_position = pl.multiple_of(seq * query_rows, query_rows)
    key_docs = doc_ref[...].astype(F32)
    query_docs = row_to_column(
        doc_ref[:, pl.ds(first_position, query_rows)].astype(F32), query_rows
    )
    key_at = lax.broadcasted_iota(jnp.int32, (query_rows, context), 1)
    query_at = first_position + lax.broadcasted_iota(jnp.int32, (query_rows, context), 0)
    open_pairs = jnp.where((key_at <= query_at) & (query_docs == key_docs), 0.0, -jnp.inf)
    context_scale = LOG2E / math.sqrt(HD)

    def attend(i, carry):
        kv_lanes = pl.ds(pl.multiple_of(i * together // groups * HD, HD), HD)
        keys = kv[:, 0, :, kv_lanes].reshape(context, HD)
        values = kv[:, 1, :, kv_lanes].reshape(context, HD)
        lanes = [
            pl.ds(pl.multiple_of((i * together + u) * HD, HD), HD) for u in range(together)
        ]
        queries = jnp.concatenate([query_buf[:, lane] for lane in lanes], axis=0)
        scores = lax.dot_general(
            queries, keys, (((1,), (1,)), ((), ())), preferred_element_type=F32
        )
        scores = scores.reshape(together, query_rows, context) + open_pairs[None]
        peak = jnp.max(scores, axis=-1, keepdims=True)
        weights = jnp.exp2((scores - peak) * context_scale)
        denominator = jnp.sum(weights, axis=-1, keepdims=True)
        output = jnp.dot(
            weights.astype(BF16).reshape(together * query_rows, context),
            values,
            preferred_element_type=F32,
        ).reshape(together, query_rows, HD)
        output = (output / denominator).astype(BF16)
        for u in range(together):
            attended_ref[:, lanes[u]] = output[u]
        return carry

    lax.fori_loop(0, heads // together, attend, 0)

    part_copy.wait_send()

    def finish_kv(j, carry):
        @pl.when((seq - 2 * j >= 0) & (seq + 2 < seqs))
        def _():
            chain_copy(j).wait_send()

        @pl.when((seq - 2 * j >= 0) & (seq - 2 * j < side))
        def _():
            side_copy(j).wait_send()

        return carry

    lax.fori_loop(0, hops, finish_kv, 0)
    keep.wait()

    def finish_out(k, carry):
        owner = lax.rem(me + k, owner_count)
        out_copy(owner).wait_send()
        pltpu.make_async_copy(
            outgoing.at[owner], delivered_hbm.at[owner], out_recv.at[owner]
        ).wait()
        return carry

    lax.fori_loop(1, owner_count, finish_out, 0)


def per_device(
    patches,
    inner_weight,
    norm_gain,
    outer_weight,
    merge_gain,
    windows,
    owners,
    context_query,
    context_key,
    context_value,
    documents,
):
    sections, seqs = lax.axis_size("section"), lax.axis_size("seq")
    owner_count = sections * seqs
    rows, width = patches.shape
    tokens = rows // 4
    capacity = max(2, 4 * tokens // owner_count)
    local = inner_weight.shape[2]
    query_rows, query_width = context_query.shape
    kv_width = context_key.shape[1]
    vmem = pl.BlockSpec(memory_space=pltpu.VMEM)
    anywhere = pl.BlockSpec(memory_space=pl.ANY)
    hops = seqs // 2
    delivered, attended = pl.pallas_call(
        functools.partial(kernel, sections, seqs, capacity),
        out_shape=(
            jax.ShapeDtypeStruct((owner_count, capacity, 2 * width), BF16),
            jax.ShapeDtypeStruct((query_rows, query_width), BF16),
        ),
        in_specs=[
            vmem,
            anywhere,
            vmem,
            anywhere,
            vmem,
            vmem,
            vmem,
            anywhere,
            anywhere,
            anywhere,
            vmem,
        ],
        out_specs=(anywhere, vmem),
        scratch_shapes=[
            pltpu.VMEM((3, width, local), BF16),
            pltpu.VMEM((local, width), BF16),
            pltpu.VMEM((query_rows, query_width), BF16),
            pltpu.VMEM((seqs, 2, query_rows, kv_width), BF16),
            pltpu.VMEM((rows, width), BF16),
            pltpu.VMEM((3, rows, local), BF16),
            pltpu.VMEM((rows, local), BF16),
            pltpu.VMEM((rows // 2, width), BF16),
            pltpu.VMEM((rows // 2, width), BF16),
            pltpu.VMEM((owner_count, capacity, 2 * width), BF16),
            pltpu.SemaphoreType.DMA((7,)),
            pltpu.SemaphoreType.DMA((seqs,)),
            pltpu.SemaphoreType.DMA((hops,)),
            pltpu.SemaphoreType.DMA((hops,)),
            pltpu.SemaphoreType.DMA((2,)),
            pltpu.SemaphoreType.DMA((owner_count,)),
            pltpu.SemaphoreType.DMA((owner_count,)),
        ],
        compiler_params=pltpu.CompilerParams(
            collective_id=0, has_side_effects=True, vmem_limit_bytes=56 * 1024 * 1024
        ),
    )(
        patches,
        inner_weight,
        norm_gain.reshape(1, width),
        outer_weight,
        merge_gain.reshape(1, width),
        windows,
        owners,
        context_query,
        context_key,
        context_value,
        documents.reshape(1, -1),
    )
    return delivered.reshape(owner_count * capacity, 2 * width), attended


def solution(mesh):
    in_specs = (
        P(("section", "seq"), None),
        P(None, None, "mp"),
        P(),
        P("mp", None),
        P(),
        P(("section", "seq"), None),
        P(("section", "seq"), None),
        P("seq", ("section", "mp")),
        P("seq", ("section", "mp")),
        P("seq", ("section", "mp")),
        P(),
    )
    out_specs = (P(("section", "seq"), "mp"), P("seq", ("section", "mp")))
    return jax.shard_map(
        per_device, mesh=mesh, in_specs=in_specs, out_specs=out_specs, check_vma=False
    )
```

```python
import functools
import math

import jax
import jax.numpy as jnp
from jax import lax
from jax.experimental import pallas as pl
from jax.experimental.pallas import tpu as pltpu
from jax.sharding import PartitionSpec as P

VD = 1280
VH = 16
QH = 64
KVH = 8
HD = 128
EPSILON = 1e-06
LOG2E = 1.4426950408889634
MESH = pl.DeviceIdType.MESH
F32 = jnp.float32
BF16 = jnp.bfloat16


def rms_scale(values, gain):
    return values * lax.rsqrt(jnp.mean(values * values, axis=-1, keepdims=True) + EPSILON) * gain


def row_to_column(row, size):
    spread = jnp.broadcast_to(row, (size, size))
    eye = lax.broadcasted_iota(jnp.int32, (size, size), 0) == lax.broadcasted_iota(
        jnp.int32, (size, size), 1
    )
    return jnp.sum(jnp.where(eye, spread, 0.0), axis=1, keepdims=True)


def kernel(
    sections,
    seqs,
    capacity,
    patches_ref,
    inner_hbm,
    norm_ref,
    outer_hbm,
    merge_ref,
    window_ref,
    owner_ref,
    query_hbm,
    key_hbm,
    value_hbm,
    doc_ref,
    delivered_hbm,
    attended_ref,
    inner_buf,
    outer_buf,
    query_buf,
    kv,
    normed_buf,
    qkv_buf,
    ctx_buf,
    part_send,
    part_recv,
    outgoing,
    load_sem,
    kv_recv,
    chain_send,
    side_send,
    part_sem,
    out_send,
    out_recv,
):
    section, seq, mp = lax.axis_index("section"), lax.axis_index("seq"), lax.axis_index("mp")
    owner_count = sections * seqs
    me = section * seqs + seq
    rows = patches_ref.shape[0]
    width = patches_ref.shape[1]
    tokens = rows // 4
    head_dim = VD // VH
    local = inner_hbm.shape[2]
    local_heads = local // head_dim
    half = rows // 2

    def at(sec, sq, m):
        return {"section": sec, "seq": sq, "mp": m}

    loads = [
        pltpu.make_async_copy(key_hbm, kv.at[seq, 0], load_sem.at[0]),
        pltpu.make_async_copy(value_hbm, kv.at[seq, 1], load_sem.at[1]),
        pltpu.make_async_copy(inner_hbm.at[0], inner_buf.at[0], load_sem.at[2]),
        pltpu.make_async_copy(inner_hbm.at[1], inner_buf.at[1], load_sem.at[3]),
        pltpu.make_async_copy(inner_hbm.at[2], inner_buf.at[2], load_sem.at[4]),
        pltpu.make_async_copy(outer_hbm, outer_buf, load_sem.at[5]),
        pltpu.make_async_copy(query_hbm, query_buf, load_sem.at[6]),
    ]
    for load in loads:
        load.start()

    barrier = pltpu.get_barrier_semaphore()

    def greet(k, carry):
        other = lax.rem(me + k, owner_count)
        pl.semaphore_signal(
            barrier,
            inc=1,
            device_id=at(other // seqs, lax.rem(other, seqs), mp),
            device_id_type=MESH,
        )
        return carry

    lax.fori_loop(1, owner_count, greet, 0)
    pl.semaphore_signal(
        barrier, inc=1, device_id=at(section, seq, 1 - mp), device_id_type=MESH
    )

    def clear(j, carry):
        kv[j] = jnp.zeros(kv.shape[1:], BF16)
        return carry

    lax.fori_loop(seq + 1, seqs, clear, 0)

    pl.semaphore_wait(barrier, owner_count)

    side = seq + 1 - 2 * lax.rem(seq, 2)

    def chain_copy(j):
        block = seq - 2 * j
        return pltpu.make_async_remote_copy(
            src_ref=kv.at[block],
            dst_ref=kv.at[block],
            send_sem=chain_send.at[j],
            recv_sem=kv_recv.at[block],
            device_id=at(section, seq + 2, mp),
            device_id_type=MESH,
        )

    def side_copy(j):
        block = seq - 2 * j
        return pltpu.make_async_remote_copy(
            src_ref=kv.at[block],
            dst_ref=kv.at[block],
            send_sem=side_send.at[j],
            recv_sem=kv_recv.at[block],
            device_id=at(section, side, mp),
            device_id_type=MESH,
        )

    def arrived(block):
        return pltpu.make_async_copy(kv.at[block], kv.at[block], kv_recv.at[block])

    loads[0].wait()
    loads[1].wait()

    @pl.when(seq + 2 < seqs)
    def _():
        chain_copy(0).start()

    @pl.when(lax.rem(seq, 2) == 0)
    def _():
        side_copy(0).start()

    def relay(j, carry):
        @pl.when(seq - 2 * j >= 0)
        def _():
            arrived(seq - 2 * j).wait()

            @pl.when(seq + 2 < seqs)
            def _():
                chain_copy(j).start()

            side_copy(j).start()

        return carry

    hops = seqs // 2
    first_hops = 1 + (hops - 1) // 3
    second_hops = 1 + 2 * (hops - 1) // 3

    normed_buf[...] = rms_scale(patches_ref[...].astype(F32), norm_ref[...].reshape(1, width)).astype(BF16)
    for i in range(3):
        loads[2 + i].wait()
        qkv_buf[i] = jnp.dot(
            normed_buf[...], inner_buf[i], preferred_element_type=F32
        ).astype(BF16)

    lax.fori_loop(1, first_hops, relay, 0)

    window_row = window_ref[...].astype(F32)
    allowed = row_to_column(window_row, rows) == window_row
    score_scale = LOG2E / math.sqrt(head_dim)
    ctx = [jnp.zeros((rows, 128), F32) for _ in range(local // 128)]
    for h in range(local_heads):
        low, high = h * head_dim, (h + 1) * head_dim
        first, last = low // 128, -(-high // 128)
        span = pl.ds(first * 128, (last - first) * 128)
        lanes = first * 128 + lax.broadcasted_iota(jnp.int32, (1, (last - first) * 128), 1)
        inside = (lanes >= low) & (lanes < high)
        query = jnp.where(inside, qkv_buf[0, :, span], jnp.zeros((), BF16))
        scores = lax.dot_general(
            query, qkv_buf[1, :, span], (((1,), (1,)), ((), ())), preferred_element_type=F32
        )
        scores = jnp.where(allowed, scores, -jnp.inf)
        peak = jnp.max(scores, axis=-1, keepdims=True)
        weights = jnp.exp2((scores - peak) * score_scale)
        denominator = jnp.sum(weights, axis=-1, keepdims=True)
        part = jnp.dot(weights.astype(BF16), qkv_buf[2, :, span], preferred_element_type=F32)
        part = jnp.where(inside, part / denominator, 0.0)
        for i in range(first, last):
            ctx[i] = ctx[i] + part[:, (i - first) * 128 : (i - first + 1) * 128]
    for i in range(local // 128):
        ctx_buf[:, i * 128 : (i + 1) * 128] = ctx[i].astype(BF16)

    lax.fori_loop(first_hops, second_hops, relay, 0)

    place = lax.broadcasted_iota(jnp.int32, (half, rows), 0)
    source_at = lax.broadcasted_iota(jnp.int32, (half, rows), 1)

    def chosen(m):
        wanted = 4 * lax.rem(place, tokens) + 2 * m + place // tokens
        return jnp.where(source_at == wanted, 1.0, 0.0).astype(BF16)

    loads[5].wait()
    their_pick = chosen(1 - mp)
    theirs = jnp.dot(their_pick, ctx_buf[...], preferred_element_type=F32).astype(BF16)
    part_copies = []
    for g in range(2):
        part_send[g] = jnp.dot(
            theirs[g * tokens : (g + 1) * tokens], outer_buf[...], preferred_element_type=F32
        ).astype(BF16)
        part_copy = pltpu.make_async_remote_copy(
            src_ref=part_send.at[g],
            dst_ref=part_recv.at[g],
            send_sem=part_sem.at[0, g],
            recv_sem=part_sem.at[1, g],
            device_id=at(section, seq, 1 - mp),
            device_id_type=MESH,
        )
        part_copy.start()
        part_copies.append(part_copy)
    pick = chosen(mp)
    ours = jnp.dot(pick, ctx_buf[...], preferred_element_type=F32).astype(BF16)
    own_part = jnp.dot(ours, outer_buf[...], preferred_element_type=F32)
    own_part = own_part + jnp.dot(pick, patches_ref[...], preferred_element_type=F32)

    owner_row = owner_ref[...].astype(F32)
    owner_spread = row_to_column(owner_row, tokens)
    earlier_at = lax.broadcasted_iota(jnp.int32, (tokens, tokens), 0)
    later_at = lax.broadcasted_iota(jnp.int32, (tokens, tokens), 1)
    rank_row = jnp.sum(
        jnp.where((owner_spread == owner_row) & (earlier_at < later_at), 1.0, 0.0),
        axis=0,
        keepdims=True,
    )
    slot_row = (owner_row * capacity + rank_row).astype(jnp.int32)
    slot_at = lax.broadcasted_iota(jnp.int32, (capacity, tokens), 0)

    lax.fori_loop(second_hops, hops, relay, 0)

    def out_copy(owner, g):
        return pltpu.make_async_remote_copy(
            src_ref=outgoing.at[g, owner],
            dst_ref=delivered_hbm.at[me, :, pl.ds(g * width, width)],
            send_sem=out_send.at[g, owner],
            recv_sem=out_recv.at[g, me],
            device_id=at(owner // seqs, lax.rem(owner, seqs), mp),
            device_id_type=MESH,
        )

    def fill(owner, g):
        spot = jnp.where(slot_at + owner * capacity == slot_row, 1.0, 0.0).astype(BF16)
        outgoing[g, owner] = jnp.dot(
            spot,
            normed_buf[g * tokens : (g + 1) * tokens, :],
            preferred_element_type=F32,
        ).astype(BF16)

    keeps = []
    for g in range(2):
        part_copies[g].wait_recv()
        residual = own_part[g * tokens : (g + 1) * tokens] + part_recv[g].astype(F32)
        normed_buf[g * tokens : (g + 1) * tokens, :] = rms_scale(
            residual, merge_ref[...].reshape(1, width)
        ).astype(BF16)

        def send_out(k, carry):
            owner = lax.rem(me + k, owner_count)
            fill(owner, g)
            out_copy(owner, g).start()
            return carry

        lax.fori_loop(1, owner_count, send_out, 0)
        fill(me, g)
        keep = pltpu.make_async_copy(
            outgoing.at[g, me],
            delivered_hbm.at[me, :, pl.ds(g * width, width)],
            out_send.at[g, me],
        )
        keep.start()
        keeps.append(keep)

    def side_arrival(j, carry):
        block = side - 2 * j

        @pl.when((block >= 0) & (block < seq))
        def _():
            arrived(block).wait()

        return carry

    lax.fori_loop(0, hops, side_arrival, 0)
    loads[6].wait()

    query_rows = query_buf.shape[0]
    context = doc_ref.shape[1]
    groups = QH // KVH
    heads = query_buf.shape[1] // HD
    together = max(1, min(4, (512 * 1024) // (query_rows * context)))
    first_position = pl.multiple_of(seq * query_rows, query_rows)
    key_docs = doc_ref[...].astype(F32)
    query_docs = row_to_column(
        doc_ref[:, pl.ds(first_position, query_rows)].astype(F32), query_rows
    )
    key_at = lax.broadcasted_iota(jnp.int32, (query_rows, context), 1)
    query_at = first_position + lax.broadcasted_iota(jnp.int32, (query_rows, context), 0)
    open_pairs = jnp.where((key_at <= query_at) & (query_docs == key_docs), 0.0, -jnp.inf)
    context_scale = LOG2E / math.sqrt(HD)

    def attend(i, carry):
        kv_lanes = pl.ds(pl.multiple_of(i * together // groups * HD, HD), HD)
        keys = kv[:, 0, :, kv_lanes].reshape(context, HD)
        values = kv[:, 1, :, kv_lanes].reshape(context, HD)
        lanes = [
            pl.ds(pl.multiple_of((i * together + u) * HD, HD), HD) for u in range(together)
        ]
        queries = jnp.concatenate([query_buf[:, lane] for lane in lanes], axis=0)
        scores = lax.dot_general(
            queries, keys, (((1,), (1,)), ((), ())), preferred_element_type=F32
        )
        scores = scores.reshape(together, query_rows, context) + open_pairs[None]
        peak = jnp.max(scores, axis=-1, keepdims=True)
        weights = jnp.exp2((scores - peak) * context_scale)
        denominator = jnp.sum(weights, axis=-1, keepdims=True)
        output = jnp.dot(
            weights.astype(BF16).reshape(together * query_rows, context),
            values,
            preferred_element_type=F32,
        ).reshape(together, query_rows, HD)
        output = (output / denominator).astype(BF16)
        for u in range(together):
            attended_ref[:, lanes[u]] = output[u]
        return carry

    lax.fori_loop(0, heads // together, attend, 0)

    for part_copy in part_copies:
        part_copy.wait_send()

    def finish_kv(j, carry):
        @pl.when((seq - 2 * j >= 0) & (seq + 2 < seqs))
        def _():
            chain_copy(j).wait_send()

        @pl.when((seq - 2 * j >= 0) & (seq - 2 * j < side))
        def _():
            side_copy(j).wait_send()

        return carry

    lax.fori_loop(0, hops, finish_kv, 0)
    for keep in keeps:
        keep.wait()

    def finish_out(k, carry):
        owner = lax.rem(me + k, owner_count)
        for g in range(2):
            out_copy(owner, g).wait_send()
            pltpu.make_async_copy(
                outgoing.at[g, owner],
                delivered_hbm.at[owner, :, pl.ds(g * width, width)],
                out_recv.at[g, owner],
            ).wait()
        return carry

    lax.fori_loop(1, owner_count, finish_out, 0)


def per_device(
    patches,
    inner_weight,
    norm_gain,
    outer_weight,
    merge_gain,
    windows,
    owners,
    context_query,
    context_key,
    context_value,
    documents,
):
    sections, seqs = lax.axis_size("section"), lax.axis_size("seq")
    owner_count = sections * seqs
    rows, width = patches.shape
    tokens = rows // 4
    capacity = max(2, 4 * tokens // owner_count)
    local = inner_weight.shape[2]
    query_rows, query_width = context_query.shape
    kv_width = context_key.shape[1]
    vmem = pl.BlockSpec(memory_space=pltpu.VMEM)
    anywhere = pl.BlockSpec(memory_space=pl.ANY)
    hops = seqs // 2
    delivered, attended = pl.pallas_call(
        functools.partial(kernel, sections, seqs, capacity),
        out_shape=(
            jax.ShapeDtypeStruct((owner_count, capacity, 2 * width), BF16),
            jax.ShapeDtypeStruct((query_rows, query_width), BF16),
        ),
        in_specs=[
            vmem,
            anywhere,
            vmem,
            anywhere,
            vmem,
            vmem,
            vmem,
            anywhere,
            anywhere,
            anywhere,
            vmem,
        ],
        out_specs=(anywhere, vmem),
        scratch_shapes=[
            pltpu.VMEM((3, width, local), BF16),
            pltpu.VMEM((local, width), BF16),
            pltpu.VMEM((query_rows, query_width), BF16),
            pltpu.VMEM((seqs, 2, query_rows, kv_width), BF16),
            pltpu.VMEM((rows, width), BF16),
            pltpu.VMEM((3, rows, local), BF16),
            pltpu.VMEM((rows, local), BF16),
            pltpu.VMEM((2, tokens, width), BF16),
            pltpu.VMEM((2, tokens, width), BF16),
            pltpu.VMEM((2, owner_count, capacity, width), BF16),
            pltpu.SemaphoreType.DMA((7,)),
            pltpu.SemaphoreType.DMA((seqs,)),
            pltpu.SemaphoreType.DMA((hops,)),
            pltpu.SemaphoreType.DMA((hops,)),
            pltpu.SemaphoreType.DMA((2, 2)),
            pltpu.SemaphoreType.DMA((2, owner_count)),
            pltpu.SemaphoreType.DMA((2, owner_count)),
        ],
        compiler_params=pltpu.CompilerParams(
            collective_id=0, has_side_effects=True, vmem_limit_bytes=56 * 1024 * 1024
        ),
    )(
        patches,
        inner_weight,
        norm_gain,
        outer_weight,
        merge_gain,
        windows,
        owners.reshape(1, tokens),
        context_query,
        context_key,
        context_value,
        documents.reshape(1, -1),
    )
    return delivered.reshape(owner_count * capacity, 2 * width), attended


def solution(mesh):
    in_specs = (
        P(("section", "seq"), None),
        P(None, None, "mp"),
        P(),
        P("mp", None),
        P(),
        P(("section", "seq"), None),
        P(("section", "seq"), None),
        P("seq", ("section", "mp")),
        P("seq", ("section", "mp")),
        P("seq", ("section", "mp")),
        P(),
    )
    out_specs = (P(("section", "seq"), "mp"), P("seq", ("section", "mp")))
    return jax.shard_map(
        per_device, mesh=mesh, in_specs=in_specs, out_specs=out_specs, check_vma=False
    )
```

```python
import functools
import math

import jax
import jax.numpy as jnp
from jax import lax
from jax.experimental import pallas as pl
from jax.experimental.pallas import tpu as pltpu
from jax.sharding import PartitionSpec as P

VD = 1280
VH = 16
QH = 64
KVH = 8
HD = 128
EPSILON = 1e-06
LOG2E = 1.4426950408889634
MESH = pl.DeviceIdType.MESH
F32 = jnp.float32
BF16 = jnp.bfloat16


def rms_scale(values, gain):
    return values * lax.rsqrt(jnp.mean(values * values, axis=-1, keepdims=True) + EPSILON) * gain


def row_to_column(row, size):
    spread = jnp.broadcast_to(row, (size, size))
    eye = lax.broadcasted_iota(jnp.int32, (size, size), 0) == lax.broadcasted_iota(
        jnp.int32, (size, size), 1
    )
    return jnp.sum(jnp.where(eye, spread, 0.0), axis=1, keepdims=True)


def kernel(
    sections,
    seqs,
    capacity,
    patches_ref,
    inner_hbm,
    norm_ref,
    outer_hbm,
    merge_ref,
    window_ref,
    owner_ref,
    query_hbm,
    key_hbm,
    value_hbm,
    doc_ref,
    delivered_hbm,
    attended_ref,
    inner_buf,
    outer_buf,
    query_buf,
    kv,
    normed_buf,
    qkv_buf,
    ctx_buf,
    part_send,
    part_recv,
    outgoing,
    load_sem,
    kv_recv,
    chain_send,
    side_send,
    part_sem,
    out_send,
    out_recv,
    relay_buf,
    slot_out,
    slot_in,
    relay_sem,
):
    section, seq, mp = lax.axis_index("section"), lax.axis_index("seq"), lax.axis_index("mp")
    owner_count = sections * seqs
    me = section * seqs + seq
    rows = patches_ref.shape[0]
    width = patches_ref.shape[1]
    tokens = rows // 4
    head_dim = VD // VH
    local = inner_hbm.shape[2]
    local_heads = local // head_dim
    half = rows // 2

    def at(sec, sq, m):
        return {"section": sec, "seq": sq, "mp": m}

    loads = [
        pltpu.make_async_copy(key_hbm, kv.at[seq, 0], load_sem.at[0]),
        pltpu.make_async_copy(value_hbm, kv.at[seq, 1], load_sem.at[1]),
        pltpu.make_async_copy(inner_hbm.at[0], inner_buf.at[0], load_sem.at[2]),
        pltpu.make_async_copy(inner_hbm.at[1], inner_buf.at[1], load_sem.at[3]),
        pltpu.make_async_copy(inner_hbm.at[2], inner_buf.at[2], load_sem.at[4]),
        pltpu.make_async_copy(outer_hbm, outer_buf, load_sem.at[5]),
        pltpu.make_async_copy(query_hbm, query_buf, load_sem.at[6]),
    ]
    for load in loads:
        load.start()

    barrier = pltpu.get_barrier_semaphore()

    def greet(k, carry):
        other = lax.rem(me + k, owner_count)
        pl.semaphore_signal(
            barrier,
            inc=1,
            device_id=at(other // seqs, lax.rem(other, seqs), mp),
            device_id_type=MESH,
        )
        return carry

    lax.fori_loop(1, owner_count, greet, 0)
    pl.semaphore_signal(
        barrier, inc=1, device_id=at(section, seq, 1 - mp), device_id_type=MESH
    )

    def clear(j, carry):
        kv[j] = jnp.zeros(kv.shape[1:], BF16)
        return carry

    lax.fori_loop(seq + 1, seqs, clear, 0)

    pl.semaphore_wait(barrier, owner_count)

    side = seq + 1 - 2 * lax.rem(seq, 2)

    def chain_copy(j):
        block = seq - 2 * j
        return pltpu.make_async_remote_copy(
            src_ref=kv.at[block],
            dst_ref=kv.at[block],
            send_sem=chain_send.at[j],
            recv_sem=kv_recv.at[block],
            device_id=at(section, seq + 2, mp),
            device_id_type=MESH,
        )

    def side_copy(j):
        block = seq - 2 * j
        return pltpu.make_async_remote_copy(
            src_ref=kv.at[block],
            dst_ref=kv.at[block],
            send_sem=side_send.at[j],
            recv_sem=kv_recv.at[block],
            device_id=at(section, side, mp),
            device_id_type=MESH,
        )

    def arrived(block):
        return pltpu.make_async_copy(kv.at[block], kv.at[block], kv_recv.at[block])

    loads[0].wait()
    loads[1].wait()

    @pl.when(seq + 2 < seqs)
    def _():
        chain_copy(0).start()

    @pl.when(lax.rem(seq, 2) == 0)
    def _():
        side_copy(0).start()

    def relay(j, carry):
        @pl.when(seq - 2 * j >= 0)
        def _():
            arrived(seq - 2 * j).wait()

            @pl.when(seq + 2 < seqs)
            def _():
                chain_copy(j).start()

            side_copy(j).start()

        return carry

    hops = seqs // 2
    first_hops = 1 + (hops - 1) // 3
    second_hops = 1 + 2 * (hops - 1) // 3

    normed_buf[...] = rms_scale(patches_ref[...].astype(F32), norm_ref[...].reshape(1, width)).astype(BF16)
    for i in range(3):
        loads[2 + i].wait()
        qkv_buf[i] = jnp.dot(
            normed_buf[...], inner_buf[i], preferred_element_type=F32
        ).astype(BF16)

    lax.fori_loop(1, first_hops, relay, 0)

    window_row = window_ref[...].astype(F32)
    allowed = row_to_column(window_row, rows) == window_row
    score_scale = LOG2E / math.sqrt(head_dim)
    ctx = [jnp.zeros((rows, 128), F32) for _ in range(local // 128)]
    for h in range(local_heads):
        low, high = h * head_dim, (h + 1) * head_dim
        first, last = low // 128, -(-high // 128)
        span = pl.ds(first * 128, (last - first) * 128)
        lanes = first * 128 + lax.broadcasted_iota(jnp.int32, (1, (last - first) * 128), 1)
        inside = (lanes >= low) & (lanes < high)
        query = jnp.where(inside, qkv_buf[0, :, span], jnp.zeros((), BF16))
        scores = lax.dot_general(
            query, qkv_buf[1, :, span], (((1,), (1,)), ((), ())), preferred_element_type=F32
        )
        scores = jnp.where(allowed, scores, -jnp.inf)
        peak = jnp.max(scores, axis=-1, keepdims=True)
        weights = jnp.exp2((scores - peak) * score_scale)
        denominator = jnp.sum(weights, axis=-1, keepdims=True)
        part = jnp.dot(weights.astype(BF16), qkv_buf[2, :, span], preferred_element_type=F32)
        part = jnp.where(inside, part / denominator, 0.0)
        for i in range(first, last):
            ctx[i] = ctx[i] + part[:, (i - first) * 128 : (i - first + 1) * 128]
    for i in range(local // 128):
        ctx_buf[:, i * 128 : (i + 1) * 128] = ctx[i].astype(BF16)

    lax.fori_loop(first_hops, second_hops, relay, 0)

    place = lax.broadcasted_iota(jnp.int32, (half, rows), 0)
    source_at = lax.broadcasted_iota(jnp.int32, (half, rows), 1)

    def chosen(m):
        wanted = 4 * lax.rem(place, tokens) + 2 * m + place // tokens
        return jnp.where(source_at == wanted, 1.0, 0.0).astype(BF16)

    loads[5].wait()
    their_pick = chosen(1 - mp)
    theirs = jnp.dot(their_pick, ctx_buf[...], preferred_element_type=F32).astype(BF16)
    part_copies = []
    for g in range(2):
        part_send[g] = jnp.dot(
            theirs[g * tokens : (g + 1) * tokens], outer_buf[...], preferred_element_type=F32
        ).astype(BF16)
        part_copy = pltpu.make_async_remote_copy(
            src_ref=part_send.at[g],
            dst_ref=part_recv.at[g],
            send_sem=part_sem.at[0, g],
            recv_sem=part_sem.at[1, g],
            device_id=at(section, seq, 1 - mp),
            device_id_type=MESH,
        )
        part_copy.start()
        part_copies.append(part_copy)
    pick = chosen(mp)
    ours = jnp.dot(pick, ctx_buf[...], preferred_element_type=F32).astype(BF16)
    own_part = jnp.dot(ours, outer_buf[...], preferred_element_type=F32)
    own_part = own_part + jnp.dot(pick, patches_ref[...], preferred_element_type=F32)

    owner_row = owner_ref[...].astype(F32)
    owner_spread = row_to_column(owner_row, tokens)
    earlier_at = lax.broadcasted_iota(jnp.int32, (tokens, tokens), 0)
    later_at = lax.broadcasted_iota(jnp.int32, (tokens, tokens), 1)
    rank_row = jnp.sum(
        jnp.where((owner_spread == owner_row) & (earlier_at < later_at), 1.0, 0.0),
        axis=0,
        keepdims=True,
    )
    slot_row = (owner_row * capacity + rank_row).astype(jnp.int32)
    slot_at = lax.broadcasted_iota(jnp.int32, (capacity, tokens), 0)

    lax.fori_loop(second_hops, hops, relay, 0)

    far_seq = lax.rem(seq + hops, seqs)
    partner = section * seqs + far_seq
    near_first = lax.div(seq, hops) * hops
    slot_out[...] = jnp.zeros(slot_out.shape, jnp.int32)
    slot_out[0:1, 0:tokens] = slot_row

    def to_partner(source, target, at_sem):
        return pltpu.make_async_remote_copy(
            src_ref=source,
            dst_ref=target,
            send_sem=relay_sem.at[0, at_sem],
            recv_sem=relay_sem.at[1, at_sem],
            device_id=at(section, far_seq, mp),
            device_id_type=MESH,
        )

    slot_copy = to_partner(slot_out, slot_in, 2)
    slot_copy.start()

    def landing(source, g):
        return delivered_hbm.at[source, :, pl.ds(g * width, width)]

    def out_copy(source, spot_at, owner, g):
        return pltpu.make_async_remote_copy(
            src_ref=outgoing.at[g, spot_at],
            dst_ref=landing(source, g),
            send_sem=out_send.at[g, spot_at],
            recv_sem=out_recv.at[g, source],
            device_id=at(owner // seqs, lax.rem(owner, seqs), mp),
            device_id_type=MESH,
        )

    def fill(slots, block, owner, spot_at, g):
        spot = jnp.where(slot_at + owner * capacity == slots, 1.0, 0.0).astype(BF16)
        outgoing[g, spot_at] = jnp.dot(spot, block, preferred_element_type=F32).astype(BF16)

    def near(k):
        sec = lax.rem(section + k, sections)
        ring = lax.rem(lax.rem(seq, hops) + lax.div(k, sections), hops)
        owner = sec * seqs + near_first + ring
        return owner, sec * seqs + lax.rem(near_first + ring + hops, seqs)

    keeps = []

    def keep_own(source, spot_at, g):
        keep = pltpu.make_async_copy(
            outgoing.at[g, spot_at], landing(source, g), out_send.at[g, spot_at]
        )
        keep.start()
        keeps.append(keep)

    relay_copies = [slot_copy]
    for g in range(2):
        part_copies[g].wait_recv()
        residual = own_part[g * tokens : (g + 1) * tokens] + part_recv[g].astype(F32)
        normed_buf[g * tokens : (g + 1) * tokens, :] = rms_scale(
            residual, merge_ref[...].reshape(1, width)
        ).astype(BF16)
        relay_copy = to_partner(
            normed_buf.at[pl.ds(g * tokens, tokens)], relay_buf.at[g], g
        )
        relay_copy.start()
        relay_copies.append(relay_copy)

        def send_out(k, carry):
            owner, _ = near(k)
            fill(slot_row, normed_buf[g * tokens : (g + 1) * tokens, :], owner, owner, g)
            out_copy(me, owner, owner, g).start()
            return carry

        lax.fori_loop(1, hops * sections, send_out, 0)
        fill(slot_row, normed_buf[g * tokens : (g + 1) * tokens, :], me, me, g)
        keep_own(me, me, g)

    slot_copy.wait_recv()
    for g in range(2):
        relay_copies[1 + g].wait_recv()

        def pass_on(k, carry):
            owner, spot_at = near(k)
            fill(slot_in[0:1, 0:tokens], relay_buf[g], owner, spot_at, g)
            out_copy(partner, spot_at, owner, g).start()
            return carry

        lax.fori_loop(1, hops * sections, pass_on, 0)
        fill(slot_in[0:1, 0:tokens], relay_buf[g], me, partner, g)
        keep_own(partner, partner, g)

    def side_arrival(j, carry):
        block = side - 2 * j

        @pl.when((block >= 0) & (block < seq))
        def _():
            arrived(block).wait()

        return carry

    lax.fori_loop(0, hops, side_arrival, 0)
    loads[6].wait()

    query_rows = query_buf.shape[0]
    context = doc_ref.shape[1]
    groups = QH // KVH
    heads = query_buf.shape[1] // HD
    together = max(1, min(4, (512 * 1024) // (query_rows * context)))
    first_position = pl.multiple_of(seq * query_rows, query_rows)
    key_docs = doc_ref[...].astype(F32)
    query_docs = row_to_column(
        doc_ref[:, pl.ds(first_position, query_rows)].astype(F32), query_rows
    )
    key_at = lax.broadcasted_iota(jnp.int32, (query_rows, context), 1)
    query_at = first_position + lax.broadcasted_iota(jnp.int32, (query_rows, context), 0)
    open_pairs = jnp.where((key_at <= query_at) & (query_docs == key_docs), 0.0, -jnp.inf)
    context_scale = LOG2E / math.sqrt(HD)

    def attend(i, carry):
        kv_lanes = pl.ds(pl.multiple_of(i * together // groups * HD, HD), HD)
        keys = kv[:, 0, :, kv_lanes].reshape(context, HD)
        values = kv[:, 1, :, kv_lanes].reshape(context, HD)
        lanes = [
            pl.ds(pl.multiple_of((i * together + u) * HD, HD), HD) for u in range(together)
        ]
        queries = jnp.concatenate([query_buf[:, lane] for lane in lanes], axis=0)
        scores = lax.dot_general(
            queries, keys, (((1,), (1,)), ((), ())), preferred_element_type=F32
        )
        scores = scores.reshape(together, query_rows, context) + open_pairs[None]
        peak = jnp.max(scores, axis=-1, keepdims=True)
        weights = jnp.exp2((scores - peak) * context_scale)
        denominator = jnp.sum(weights, axis=-1, keepdims=True)
        output = jnp.dot(
            weights.astype(BF16).reshape(together * query_rows, context),
            values,
            preferred_element_type=F32,
        ).reshape(together, query_rows, HD)
        output = (output / denominator).astype(BF16)
        for u in range(together):
            attended_ref[:, lanes[u]] = output[u]
        return carry

    lax.fori_loop(0, heads // together, attend, 0)

    for part_copy in part_copies:
        part_copy.wait_send()

    def finish_kv(j, carry):
        @pl.when((seq - 2 * j >= 0) & (seq + 2 < seqs))
        def _():
            chain_copy(j).wait_send()

        @pl.when((seq - 2 * j >= 0) & (seq - 2 * j < side))
        def _():
            side_copy(j).wait_send()

        return carry

    lax.fori_loop(0, hops, finish_kv, 0)
    for keep in keeps:
        keep.wait()

    for relay_copy in relay_copies:
        relay_copy.wait_send()

    def finish_out(k, carry):
        owner, spot_at = near(k)
        for g in range(2):
            out_copy(me, owner, owner, g).wait_send()
            out_copy(partner, spot_at, owner, g).wait_send()
            for source in (owner, spot_at):
                pltpu.make_async_copy(
                    outgoing.at[g, source], landing(source, g), out_recv.at[g, source]
                ).wait()
        return carry

    lax.fori_loop(1, hops * sections, finish_out, 0)


def per_device(
    patches,
    inner_weight,
    norm_gain,
    outer_weight,
    merge_gain,
    windows,
    owners,
    context_query,
    context_key,
    context_value,
    documents,
):
    sections, seqs = lax.axis_size("section"), lax.axis_size("seq")
    owner_count = sections * seqs
    rows, width = patches.shape
    tokens = rows // 4
    capacity = max(2, 4 * tokens // owner_count)
    local = inner_weight.shape[2]
    query_rows, query_width = context_query.shape
    kv_width = context_key.shape[1]
    vmem = pl.BlockSpec(memory_space=pltpu.VMEM)
    anywhere = pl.BlockSpec(memory_space=pl.ANY)
    hops = seqs // 2
    delivered, attended = pl.pallas_call(
        functools.partial(kernel, sections, seqs, capacity),
        out_shape=(
            jax.ShapeDtypeStruct((owner_count, capacity, 2 * width), BF16),
            jax.ShapeDtypeStruct((query_rows, query_width), BF16),
        ),
        in_specs=[
            vmem,
            anywhere,
            vmem,
            anywhere,
            vmem,
            vmem,
            vmem,
            anywhere,
            anywhere,
            anywhere,
            vmem,
        ],
        out_specs=(anywhere, vmem),
        scratch_shapes=[
            pltpu.VMEM((3, width, local), BF16),
            pltpu.VMEM((local, width), BF16),
            pltpu.VMEM((query_rows, query_width), BF16),
            pltpu.VMEM((seqs, 2, query_rows, kv_width), BF16),
            pltpu.VMEM((rows, width), BF16),
            pltpu.VMEM((3, rows, local), BF16),
            pltpu.VMEM((rows, local), BF16),
            pltpu.VMEM((2, tokens, width), BF16),
            pltpu.VMEM((2, tokens, width), BF16),
            pltpu.VMEM((2, owner_count, capacity, width), BF16),
            pltpu.SemaphoreType.DMA((7,)),
            pltpu.SemaphoreType.DMA((seqs,)),
            pltpu.SemaphoreType.DMA((hops,)),
            pltpu.SemaphoreType.DMA((hops,)),
            pltpu.SemaphoreType.DMA((2, 2)),
            pltpu.SemaphoreType.DMA((2, owner_count)),
            pltpu.SemaphoreType.DMA((2, owner_count)),
            pltpu.VMEM((2, tokens, width), BF16),
            pltpu.VMEM((8, 128), jnp.int32),
            pltpu.VMEM((8, 128), jnp.int32),
            pltpu.SemaphoreType.DMA((2, 3)),
        ],
        compiler_params=pltpu.CompilerParams(
            collective_id=0, has_side_effects=True, vmem_limit_bytes=56 * 1024 * 1024
        ),
    )(
        patches,
        inner_weight,
        norm_gain,
        outer_weight,
        merge_gain,
        windows,
        owners.reshape(1, tokens),
        context_query,
        context_key,
        context_value,
        documents.reshape(1, -1),
    )
    return delivered.reshape(owner_count * capacity, 2 * width), attended


def solution(mesh):
    in_specs = (
        P(("section", "seq"), None),
        P(None, None, "mp"),
        P(),
        P("mp", None),
        P(),
        P(("section", "seq"), None),
        P(("section", "seq"), None),
        P("seq", ("section", "mp")),
        P("seq", ("section", "mp")),
        P("seq", ("section", "mp")),
        P(),
    )
    out_specs = (P(("section", "seq"), "mp"), P("seq", ("section", "mp")))
    return jax.shard_map(
        per_device, mesh=mesh, in_specs=in_specs, out_specs=out_specs, check_vma=False
    )
```
